32 devices in a mesh: col: 4 (over y, x), gz: 8 (over z, core).
Axes of the slice: x: 2, y: 2, z: 4, core: 2. Of those that a mesh axis runs over, the one named last changes fastest.
Arguments:
- segments: float32 [9, 98304], P(None, ('col', 'gz')), may hold values from -6 to 6
- node_owner: int32 [2, 98304], P(None, ('col', 'gz')), may hold values from 0 to 4
- node_slot: int32 [2, 98304], P(None, ('col', 'gz')), may hold values from 0 to 3071
- pair_first: int32 [10240], P(('col', 'gz')), may hold values from 0 to 23
- pair_second: int32 [10240], P(('col', 'gz')), may hold values from 0 to 71
- pair_count: int32 [32], P(('col', 'gz')), may hold values from 106 to 320, as said below
Outputs:
- node_force: float32 [3, 98304], P(None, ('col', 'gz'))
The draws below stay inside these ranges and needn't reach their ends.
Inputs may be any that keep to these rules, and one draw needn't show every extreme that they name: `pair_count`: each device has at least 106 listed pairs (a third, rounded down), and some device has exactly 320; entries past a device's count are ignored.
All inputs are finite; a program needn't handle non-finite values.
Results may differ from the reference program's by a relative error of at most 0.0003.
Values sent between devices are 32-bit elements; how exact they have to be, the bound alone decides.
No kernel may reach another device: no remote copies, remote signals or barrier semaphores. Data moves between devices by JAX's collectives and lax.ppermute only.
A program may use at most 64 MiB of HBM per device.

```python
import jax
import jax.numpy as jnp
from jax import lax

BLK = 128
SEG_DEV = 3072
MAXP = 320
NB_DEV = 24
NODE_DEV = 3072
DEVS = 32
SEGS = 98304
NODES = 98304
PAIRS = 10240
GRIDX = 1
N_COL = 4
N_GZ = 8


def draw_pair_count(key, part):
    first_key, second_key = jax.random.split(key)
    counts = jax.random.randint(first_key, (DEVS,), MAXP // 3, MAXP + 1)
    chosen = jax.random.randint(second_key, (), 0, DEVS)
    return jnp.where(jnp.arange(DEVS) == chosen, MAXP, counts).astype(jnp.int32)


def plant(entries, key, low, largest):
    extent = entries.shape
    place = [jax.random.randint(jax.random.fold_in(key, axis), (), 0, extent[axis]) for axis in range(len(extent))]
    entries = entries.at[tuple(place)].set(low)
    longest = extent.index(max(extent))
    place[longest] = (place[longest] + 1) % extent[longest]
    return entries.at[tuple(place)].set(largest)


def block_scale(rng, dims, cuts, least, high):
    gain = 1.0
    for axis_at, parts in cuts:
        draws = jax.random.uniform(jax.random.fold_in(jax.random.fold_in(rng, 6), axis_at), (parts,), jnp.float32, least / len(cuts), high / len(cuts))
        gain = gain * jnp.repeat(jnp.exp(draws), dims[axis_at] // parts).reshape((-1,) + (1,) * (len(dims) - 1 - axis_at))
    return gain


def normal_values(rng, shape, spread, bound, cuts=(), held_as=jnp.bfloat16):
    result = spread * jax.random.normal(rng, shape, jnp.float32)
    if cuts:
        result = result * block_scale(rng, shape, cuts, -0.22, 0.18)
    return jnp.clip(result, -bound, bound).astype(held_as)


def setup_inputs(seed: int = 0) -> dict:
    key_of = jax.random.split(jax.random.key(seed), 7)
    segments = normal_values(key_of[0], (9, SEGS), 1.0, 6.0, ((1, 32),), jnp.float32)
    node_owner = plant(jax.random.randint(key_of[1], (2, SEGS), 0, 5), jax.random.fold_in(key_of[1], 1), 0, 4).astype(jnp.int32)
    node_slot = plant(jax.random.randint(key_of[2], (2, SEGS), 0, NODE_DEV), jax.random.fold_in(key_of[2], 1), 0, NODE_DEV - 1).astype(jnp.int32)
    pair_first = plant(jax.random.randint(key_of[3], (PAIRS,), 0, NB_DEV), jax.random.fold_in(key_of[3], 1), 0, NB_DEV - 1).astype(jnp.int32)
    pair_second = plant(jax.random.randint(key_of[4], (PAIRS,), 0, 3 * NB_DEV), jax.random.fold_in(key_of[4], 1), 0, (3 * NB_DEV) - 1).astype(jnp.int32)
    pair_count = draw_pair_count(jax.random.fold_in(key_of[6], 71), 0)
    return dict(segments=segments, node_owner=node_owner, node_slot=node_slot, pair_first=pair_first, pair_second=pair_second, pair_count=pair_count)


MU = 0.02
CORE_SQ = 0.5

def pair_tile(first_block, second_block):
    first_pos = first_block[0:3]
    second_pos = second_block[0:3]
    offset = first_pos[:, :, None] - second_pos[:, None, :]
    radius_sq = lax.optimization_barrier(jnp.sum(offset * offset, axis=0)) + CORE_SQ
    inverse = lax.rsqrt(radius_sq)
    burgers = jnp.dot(first_block[3:6].T, second_block[3:6], precision=lax.Precision.HIGHEST, preferred_element_type=jnp.float32)
    tangents = jnp.dot(first_block[6:9].T, second_block[6:9], precision=lax.Precision.HIGHEST, preferred_element_type=jnp.float32)
    coupling = MU * burgers * tangents * (inverse * inverse * inverse)
    pulled = jnp.einsum('kj,ij->ki', second_pos, coupling, precision=lax.Precision.HIGHEST)
    return first_pos * lax.optimization_barrier(jnp.sum(coupling, axis=1))[None, :] - pulled

def reference(segments, node_owner, node_slot, pair_first, pair_second, pair_count):
    by_device = segments.reshape(9, N_COL, N_GZ, SEG_DEV)
    firsts_all = pair_first.reshape(DEVS, MAXP)
    seconds_all = pair_second.reshape(DEVS, MAXP)
    owners_all = node_owner.reshape(2, DEVS, SEG_DEV)
    slots_all = node_slot.reshape(2, DEVS, SEG_DEV)

    def per_device(device):
        column = device // N_GZ
        layer_index = device % N_GZ
        below = by_device[:, column, (layer_index - 1) % N_GZ]
        center = by_device[:, column, layer_index]
        above = by_device[:, column, (layer_index + 1) % N_GZ]
        window = jnp.concatenate([below, center, above], axis=1)
        firsts = firsts_all[device]
        seconds = seconds_all[device]
        active = (jnp.arange(MAXP, dtype=jnp.int32) < pair_count[device]).astype(jnp.float32)
        first_blocks = jax.vmap(lambda block_index: lax.dynamic_slice_in_dim(center, block_index * BLK, BLK, 1))(firsts)
        second_blocks = jax.vmap(lambda block_index: lax.dynamic_slice_in_dim(window, block_index * BLK, BLK, 1))(seconds)
        tile_forces = jax.vmap(pair_tile)(first_blocks, second_blocks) * active[:, None, None]
        forces = jnp.zeros((3, NB_DEV, BLK), jnp.float32).at[:, firsts].add(jnp.transpose(tile_forces, (1, 0, 2)))
        halved = 0.5 * forces.reshape(3, SEG_DEV)
        owners = owners_all[:, device]
        slots = slots_all[:, device]
        buffer = jnp.zeros((3, 5 * NODE_DEV), jnp.float32)
        buffer = buffer.at[:, owners[0] * NODE_DEV + slots[0]].add(halved)
        buffer = buffer.at[:, owners[1] * NODE_DEV + slots[1]].add(halved)
        return buffer.reshape(3, 5, NODE_DEV)
    partials = lax.map(per_device, jnp.arange(DEVS, dtype=jnp.int32))
    partials = partials.reshape(N_COL, N_GZ, 3, 5, NODE_DEV)
    node_total = partials[:, :, :, 0]
    node_total = node_total + jnp.roll(partials[:, :, :, 1], 1, axis=0)
    node_total = node_total + jnp.roll(partials[:, :, :, 2], -1, axis=0)
    node_total = node_total + jnp.roll(partials[:, :, :, 3], GRIDX, axis=0)
    node_total = node_total + jnp.roll(partials[:, :, :, 4], -GRIDX, axis=0)
    return jnp.transpose(node_total, (2, 0, 1, 3)).reshape(3, NODES)
```

```python
import functools

import jax
import jax.numpy as jnp
from jax import lax
from jax.experimental import pallas as pl
from jax.experimental.pallas import tpu as pltpu
from jax.sharding import PartitionSpec as P

BLK = 128
NODE_DEV = 3072
MU = 0.02
CORE_SQ = 0.5

ROWS = 64
MOM = 16
GROUP = 32
TAIL = 16
BF = jnp.bfloat16
F32 = jnp.float32

_TN = (((0,), (0,)), ((), ()))
_NT = (((1,), (1,)), ((), ()))


def split3(v):
    a = v.astype(BF).astype(F32)
    r = v - a
    b = r.astype(BF).astype(F32)
    return a, b, r - b


def gather_components(seg_ref, comp, blocks):
    for b in range(blocks):
        lanes = slice(b * BLK, (b + 1) * BLK)
        comp[pl.ds(b, 8, stride=blocks), :] = seg_ref[0:8, lanes]
        comp[8 * blocks + b : 8 * blocks + b + 1, :] = seg_ref[8:9, lanes]


def features(comp, blocks):
    part = [comp[c * blocks : (c + 1) * blocks, :] for c in range(9)]
    x, burgers, line = part[0:3], part[3:6], part[6:9]
    xs = [split3(v) for v in x]
    norm = x[0] * x[0] + x[1] * x[1] + x[2] * x[2]
    prods = [split3(p * q)[0:1] + (p * q,) for p in burgers for q in line]
    prods = [(hi, full - hi) for hi, full in prods]
    return xs, norm, prods


def source_rows(xs, norm, prods):
    one = jnp.ones_like(norm)
    rows = {}
    norms = split3(norm + CORE_SQ)
    for k in range(3):
        x1, x2, x3 = xs[k]
        rows[k], rows[3 + k], rows[6 + k] = x1, x2, x3
        rows[9 + k], rows[12 + k] = one, norms[k]
        rows[15 + k], rows[18 + k], rows[21 + k] = x1, x2, x1
    for m, (hi, lo) in enumerate(prods):
        rows[32 + m], rows[41 + m], rows[50 + m] = hi, lo, hi
    return rows


def target_rows(xs, norm, prods):
    one = jnp.ones_like(norm)
    rows = {}
    norms = split3(norm)
    for k in range(3):
        x1, x2, x3 = (-2.0 * v for v in xs[k])
        rows[k], rows[3 + k], rows[6 + k] = x1, x1, x1
        rows[9 + k], rows[12 + k] = norms[k], one
        rows[15 + k], rows[18 + k], rows[21 + k] = x2, x2, x3
    for m, (hi, lo) in enumerate(prods):
        rows[32 + m], rows[41 + m], rows[50 + m] = hi, hi, lo
    return rows


def put_rows(rows, feat, blocks):
    for r in range(ROWS):
        feat[r * blocks : (r + 1) * blocks, :] = rows.get(r, jnp.zeros((blocks, BLK), F32))


def block_rows(feat, b, blocks):
    return feat[pl.ds(b, ROWS, stride=blocks), :].astype(BF)


def source_table(comp, feat, table, base, blocks):
    put_rows(source_rows(*features(comp, blocks)), feat, blocks)
    for b in range(blocks):
        table[base + b] = block_rows(feat, b, blocks)


def empty_block(table, at):
    row = lax.broadcasted_iota(jnp.int32, (ROWS, BLK), 0)
    table[at] = jnp.where(row == 12, 1.0, 0.0).astype(BF)


def pair_group(count, start, entry, target, source, forces):
    codes = [entry(start + u) for u in range(count)]
    both = [
        lax.dot_general(source[c & 127], target[c >> 7], _TN, preferred_element_type=F32)
        for c in codes
    ]
    weights = []
    for value in both:
        inverse = lax.rsqrt(value[:, :BLK])
        coupling = value[:, BLK:] * inverse * (inverse * inverse)
        hi = coupling.astype(BF)
        lo = (coupling - hi.astype(F32)).astype(BF)
        weights.append(jnp.concatenate([hi, lo], axis=0))
    for c, weight in zip(codes, weights):
        moment = source[c & 127, 0:MOM, :]
        moment = jnp.concatenate([moment, moment], axis=1)
        forces[c >> 7] += jnp.dot(moment, weight, preferred_element_type=F32)


def all_pairs(total, entry, target, source, forces):
    whole = (total + (GROUP - TAIL - 1)) // GROUP

    def step(q, carry):
        pair_group(GROUP, q * GROUP, entry, target, source, forces)
        return carry

    lax.fori_loop(0, whole, step, 0)

    @pl.when(whole * GROUP < total)
    def _():
        pair_group(TAIL, whole * GROUP, entry, target, source, forces)


def own_kernel(
    blocks, first_ref, second_ref, count_ref, seg_ref,
    target_ref, comp_ref, forces_ref, halo_list, halo_total,
    feat, source, own_list,
):
    slots = first_ref.shape[0]
    total = count_ref[0]
    empty = blocks

    def sort(p, carry):
        n_own, n_halo = carry
        first, second = first_ref[p], second_ref[p]
        own = jnp.logical_and(second >= blocks, second < 2 * blocks).astype(jnp.int32)
        listed = (p < total).astype(jnp.int32)
        shifted = second - jnp.where(second >= blocks, blocks, 0)
        code = first * 128 + shifted
        own_list[n_own] = code
        halo_list[n_halo] = code
        return n_own + own * listed, n_halo + (1 - own) * listed

    n_own, n_halo = lax.fori_loop(0, slots, sort, (0, 0), unroll=8 if slots % 8 == 0 else 1)
    for u in range(GROUP):
        own_list[n_own + u] = empty
        halo_list[n_halo + u] = 2 * blocks
    halo_total[0] = n_halo

    gather_components(seg_ref, comp_ref, blocks)
    parts = features(comp_ref, blocks)
    put_rows(source_rows(*parts), feat, blocks)
    for b in range(blocks):
        source[b] = block_rows(feat, b, blocks)
    empty_block(source, empty)
    xs, norm, prods = parts
    part = [comp_ref[c * blocks : (c + 1) * blocks, :] for c in range(3, 9)]
    scaled = [MU * p * q for p in part[0:3] for q in part[3:6]]
    scaled = [(split3(v)[0], v) for v in scaled]
    scaled = [(hi, full - hi) for hi, full in scaled]
    put_rows(target_rows(xs, norm, scaled), feat, blocks)
    blank = jnp.zeros((ROWS // 2, BLK), BF)
    for b in range(blocks):
        rows = block_rows(feat, b, blocks)
        target_ref[b, 0:32, 0:BLK] = rows[0:32]
        target_ref[b, 0:32, BLK:] = blank
        target_ref[b, 32:64, 0:BLK] = blank
        target_ref[b, 32:64, BLK:] = rows[32:64]

    forces_ref[...] = jnp.zeros_like(forces_ref)
    all_pairs(n_own, lambda p: own_list[p], target_ref, source, forces_ref)


def halo_kernel(
    blocks, codes_to, targets, halo_list, halo_total, below_ref, above_ref, target_ref, comp_ref, own_forces,
    owner_ref, slot_ref, *rest,
):
    outs, (comp, feat, source, forces, scaled, left, right, total) = rest[:targets], rest[targets:]
    for base, seg_ref in ((0, below_ref), (blocks, above_ref)):
        gather_components(seg_ref, comp, blocks)
        source_table(comp, feat, source, base, blocks)
    empty_block(source, 2 * blocks)
    forces[...] = own_forces[...]
    all_pairs(halo_total[0], lambda p: halo_list[p], target_ref, source, forces)

    flat = forces.reshape(blocks * MOM, BLK)
    row = [flat[pl.ds(m, blocks, stride=MOM), :] for m in range(10)]
    for k in range(3):
        pulled = row[k] + row[3 + k] + row[6 + k]
        half = 0.5 * (comp_ref[k * blocks : (k + 1) * blocks, :] * row[9] - pulled)
        hi = half.astype(BF).astype(F32)
        scaled[k * blocks : (k + 1) * blocks, :] = hi
        scaled[(3 + k) * blocks : (4 + k) * blocks, :] = half - hi

    highs = NODE_DEV // BLK
    span = targets * highs
    codes = owner_ref[...]
    place = jnp.zeros_like(codes)
    for code, to in enumerate(codes_to):
        if to:
            place = jnp.where(codes == code, to, place)
    slot = slot_ref[...]
    high = place * highs + (slot >> 7)
    low = slot & 127
    high_at = lax.broadcasted_iota(jnp.int32, (span, BLK), 0)
    low_at = lax.broadcasted_iota(jnp.int32, (BLK, BLK), 0)
    for b in range(blocks):
        lanes = slice(b * BLK, (b + 1) * BLK)
        values = [scaled[m * blocks + b : m * blocks + b + 1, :] for m in range(6)]
        for end in range(2):
            at = slice((2 * b + end) * BLK, (2 * b + end + 1) * BLK)
            hit = high_at == high[end : end + 1, lanes]
            right[:, at] = jnp.where(low_at == low[end : end + 1, lanes], 1.0, 0.0).astype(BF)
            for m in range(6):
                left[m * span : (m + 1) * span, at] = jnp.where(hit, values[m], 0.0).astype(BF)
    summed = lax.dot_general(left[...], right[...], _NT, preferred_element_type=F32)
    total[...] = summed[: 3 * span] + summed[3 * span :]
    for t, out in enumerate(outs):
        for h in range(highs):
            out[:, h * BLK : (h + 1) * BLK] = total[pl.ds(t * highs + h, 3, stride=span), :]


def on_device(segments, node_owner, node_slot, pair_first, pair_second, pair_count):
    width = segments.shape[1]
    blocks = width // BLK
    slots = pair_first.shape[0]
    peers = lax.axis_size("gz")
    up = [(i, (i + 1) % peers) for i in range(peers)]
    down = [(j, i) for i, j in up]
    below = lax.ppermute(segments, "gz", up)
    above = lax.ppermute(segments, "gz", down)

    smem = pl.BlockSpec(memory_space=pltpu.SMEM)
    vmem = pl.BlockSpec(memory_space=pltpu.VMEM)
    params = pltpu.CompilerParams(vmem_limit_bytes=40 << 20)
    table, comp, forces, halo_list, halo_total = pl.pallas_call(
        functools.partial(own_kernel, blocks),
        out_shape=(
            jax.ShapeDtypeStruct((blocks, ROWS, 2 * BLK), BF),
            jax.ShapeDtypeStruct((9 * blocks, BLK), F32),
            jax.ShapeDtypeStruct((blocks, MOM, BLK), F32),
            jax.ShapeDtypeStruct((slots + GROUP,), jnp.int32),
            jax.ShapeDtypeStruct((1,), jnp.int32),
        ),
        in_specs=[smem, smem, smem, vmem],
        out_specs=(vmem, vmem, vmem, smem, smem),
        scratch_shapes=[
            pltpu.VMEM((ROWS * blocks, BLK), F32),
            pltpu.VMEM((blocks + 1, ROWS, BLK), BF),
            pltpu.SMEM((slots + GROUP,), jnp.int32),
        ],
        compiler_params=params,
        cost_estimate=pl.CostEstimate(flops=10_000_000_000, bytes_accessed=1_000_000, transcendentals=0),
    )(pair_first, pair_second, pair_count, segments)

    columns = lax.axis_size("col")
    stride = columns // 4
    moves = [m % columns for m in (0, 1, -1, stride, -stride)]
    shifts = list(dict.fromkeys(moves))
    targets = len(shifts)
    span = targets * (NODE_DEV // BLK)
    partials = pl.pallas_call(
        functools.partial(halo_kernel, blocks, [shifts.index(m) for m in moves], targets),
        out_shape=tuple(jax.ShapeDtypeStruct((3, NODE_DEV), F32) for _ in shifts),
        in_specs=[smem, smem] + [vmem] * 7,
        out_specs=(vmem,) * targets,
        scratch_shapes=[
            pltpu.VMEM((9 * blocks, BLK), F32),
            pltpu.VMEM((ROWS * blocks, BLK), F32),
            pltpu.VMEM((2 * blocks + 1, ROWS, BLK), BF),
            pltpu.VMEM((blocks, MOM, BLK), F32),
            pltpu.VMEM((6 * blocks, BLK), F32),
            pltpu.VMEM((6 * span, 2 * width), BF),
            pltpu.VMEM((BLK, 2 * width), BF),
            pltpu.VMEM((3 * span, BLK), F32),
        ],
        compiler_params=params,
    )(halo_list, halo_total, below, above, table, comp, forces, node_owner, node_slot)
    node_total = partials[0]
    for shift, partial in zip(shifts[1:], partials[1:]):
        node_total = node_total + lax.ppermute(partial, "col", [(i, (i + shift) % columns) for i in range(columns)])
    return node_total


def solution(mesh):
    in_specs = (
        P(None, ("col", "gz")),
        P(None, ("col", "gz")),
        P(None, ("col", "gz")),
        P(("col", "gz")),
        P(("col", "gz")),
        P(("col", "gz")),
    )
    out_specs = P(None, ("col", "gz"))
    return jax.shard_map(
        on_device, mesh=mesh, in_specs=in_specs, out_specs=out_specs, check_vma=False
    )
```

```python
import functools

import jax
import jax.numpy as jnp
from jax import lax
from jax.experimental import pallas as pl
from jax.experimental.pallas import tpu as pltpu
from jax.sharding import PartitionSpec as P

BLK = 128
NODE_DEV = 3072
MU = 0.02
CORE_SQ = 0.5

ROWS = 64
MOM = 16
GROUP = 32
TAIL = 16
BF = jnp.bfloat16
F32 = jnp.float32

_TN = (((0,), (0,)), ((), ()))
_NT = (((1,), (1,)), ((), ()))


def split3(v):
    a = v.astype(BF).astype(F32)
    r = v - a
    b = r.astype(BF).astype(F32)
    return a, b, r - b


def gather_components(seg_ref, comp, blocks):
    for b in range(blocks):
        lanes = slice(b * BLK, (b + 1) * BLK)
        comp[pl.ds(b, 8, stride=blocks), :] = seg_ref[0:8, lanes]
        comp[8 * blocks + b : 8 * blocks + b + 1, :] = seg_ref[8:9, lanes]


def features(comp, blocks):
    part = [comp[c * blocks : (c + 1) * blocks, :] for c in range(9)]
    x, burgers, line = part[0:3], part[3:6], part[6:9]
    xs = [split3(v) for v in x]
    norm = x[0] * x[0] + x[1] * x[1] + x[2] * x[2]
    prods = [split3(p * q)[0:1] + (p * q,) for p in burgers for q in line]
    prods = [(hi, full - hi) for hi, full in prods]
    return xs, norm, prods


def source_rows(xs, norm, prods):
    one = jnp.ones_like(norm)
    rows = {}
    norms = split3(norm + CORE_SQ)
    for k in range(3):
        x1, x2, x3 = xs[k]
        rows[k], rows[3 + k], rows[6 + k] = x1, x2, x3
        rows[9 + k], rows[12 + k] = one, norms[k]
        rows[15 + k], rows[18 + k], rows[21 + k] = x1, x2, x1
    for m, (hi, lo) in enumerate(prods):
        rows[32 + m], rows[41 + m], rows[50 + m] = hi, lo, hi
    return rows


def target_rows(xs, norm, prods):
    one = jnp.ones_like(norm)
    rows = {}
    norms = split3(norm)
    for k in range(3):
        x1, x2, x3 = (-2.0 * v for v in xs[k])
        rows[k], rows[3 + k], rows[6 + k] = x1, x1, x1
        rows[9 + k], rows[12 + k] = norms[k], one
        rows[15 + k], rows[18 + k], rows[21 + k] = x2, x2, x3
    for m, (hi, lo) in enumerate(prods):
        rows[32 + m], rows[41 + m], rows[50 + m] = hi, hi, lo
    return rows


def put_rows(rows, feat, blocks):
    for r in range(ROWS):
        feat[r * blocks : (r + 1) * blocks, :] = rows.get(r, jnp.zeros((blocks, BLK), F32))


def block_rows(feat, b, blocks):
    return feat[pl.ds(b, ROWS, stride=blocks), :].astype(BF)


def source_table(comp, feat, table, base, blocks):
    put_rows(source_rows(*features(comp, blocks)), feat, blocks)
    for b in range(blocks):
        table[base + b] = block_rows(feat, b, blocks)


def empty_block(table, at):
    row = lax.broadcasted_iota(jnp.int32, (ROWS, BLK), 0)
    table[at] = jnp.where(row == 12, 1.0, 0.0).astype(BF)


def pair_group(count, start, entry, target, source, forces):
    codes = [entry(start + u) for u in range(count)]
    both = [
        lax.dot_general(source[c & 127], target[c >> 7], _TN, preferred_element_type=F32)
        for c in codes
    ]
    weights = []
    for value in both:
        inverse = lax.rsqrt(value[:, :BLK])
        coupling = value[:, BLK:] * inverse * (inverse * inverse)
        hi = coupling.astype(BF)
        lo = (coupling - hi.astype(F32)).astype(BF)
        weights.append(jnp.concatenate([hi, lo], axis=0))
    for c, weight in zip(codes, weights):
        moment = source[c & 127, 0:MOM, :]
        moment = jnp.concatenate([moment, moment], axis=1)
        forces[c >> 7] += jnp.dot(moment, weight, preferred_element_type=F32)


def all_pairs(total, entry, target, source, forces):
    whole = (total + (GROUP - TAIL - 1)) // GROUP

    def step(q, carry):
        pair_group(GROUP, q * GROUP, entry, target, source, forces)
        return carry

    lax.fori_loop(0, whole, step, 0)

    @pl.when(whole * GROUP < total)
    def _():
        pair_group(TAIL, whole * GROUP, entry, target, source, forces)


def sort_pairs(blocks, packed, lists):
    slots, places = packed.shape[1], lists.shape[1]
    listed = packed >= 0
    first, second = packed >> 7, packed & 127
    inside = jnp.logical_and(second >= blocks, second < 2 * blocks)
    own = jnp.where(jnp.logical_and(listed, inside), 1.0, 0.0)
    halo = jnp.where(listed, 1.0, 0.0) - own
    line = lax.broadcasted_iota(jnp.int32, (16, slots), 0)
    member = jnp.where(line == 0, own, jnp.where(line == 1, halo, 0.0)).astype(BF)
    before = lax.broadcasted_iota(jnp.int32, (slots, slots), 0) < lax.broadcasted_iota(jnp.int32, (slots, slots), 1)
    rank = jnp.dot(member, jnp.where(before, 1.0, 0.0).astype(BF), preferred_element_type=F32)
    source = second - jnp.where(second >= blocks, blocks, 0)
    value = jnp.where(line == 0, first, jnp.where(line == 1, source, 0)).astype(F32).astype(BF)
    place = lax.broadcasted_iota(jnp.int32, (places, slots), 0).astype(F32)
    for r, (mine, empty) in enumerate(((own, blocks), (halo, 2 * blocks))):
        at = jnp.where(mine > 0.0, rank[r : r + 1], -1.0)
        hit = jnp.where(place == at, 1.0, 0.0).astype(BF)
        found = lax.dot_general(value, hit, _NT, preferred_element_type=F32)
        code = (found[0:1] * 128.0 + found[1:2]).astype(jnp.int32)
        total = jnp.sum(mine, axis=1, keepdims=True).astype(jnp.int32)
        lane = lax.broadcasted_iota(jnp.int32, (1, places), 1)
        lists[r : r + 1, :] = jnp.where(lane < total, code, empty)
        lists[2 + r : 3 + r, :] = jnp.broadcast_to(total, (1, places))


def own_kernel(
    blocks, packed_ref, seg_ref,
    target_ref, comp_ref, forces_ref, lists_ref,
    feat, source, lists, done,
):
    empty = blocks
    sort_pairs(blocks, packed_ref[...].reshape(1, packed_ref.shape[0]), lists)
    copy = pltpu.make_async_copy(lists, lists_ref, done.at[1])
    copy.start()

    gather_components(seg_ref, comp_ref, blocks)
    parts = features(comp_ref, blocks)
    put_rows(source_rows(*parts), feat, blocks)
    for b in range(blocks):
        source[b] = block_rows(feat, b, blocks)
    empty_block(source, empty)
    xs, norm, prods = parts
    part = [comp_ref[c * blocks : (c + 1) * blocks, :] for c in range(3, 9)]
    scaled = [MU * p * q for p in part[0:3] for q in part[3:6]]
    scaled = [(split3(v)[0], v) for v in scaled]
    scaled = [(hi, full - hi) for hi, full in scaled]
    put_rows(target_rows(xs, norm, scaled), feat, blocks)
    blank = jnp.zeros((ROWS // 2, BLK), BF)
    for b in range(blocks):
        rows = block_rows(feat, b, blocks)
        target_ref[b, 0:32, 0:BLK] = rows[0:32]
        target_ref[b, 0:32, BLK:] = blank
        target_ref[b, 32:64, 0:BLK] = blank
        target_ref[b, 32:64, BLK:] = rows[32:64]

    forces_ref[...] = jnp.zeros_like(forces_ref)
    copy.wait()
    all_pairs(lists_ref[2, 0], lambda p: lists_ref[0, p], target_ref, source, forces_ref)


def halo_kernel(
    blocks, codes_to, targets, lists_ref, below_ref, above_ref, target_ref, comp_ref, own_forces,
    owner_ref, slot_ref, *rest,
):
    outs, (comp, feat, source, forces, scaled, left, right, total) = rest[:targets], rest[targets:]
    for base, seg_ref in ((0, below_ref), (blocks, above_ref)):
        gather_components(seg_ref, comp, blocks)
        source_table(comp, feat, source, base, blocks)
    empty_block(source, 2 * blocks)
    forces[...] = own_forces[...]
    all_pairs(lists_ref[3, 0], lambda p: lists_ref[1, p], target_ref, source, forces)

    flat = forces.reshape(blocks * MOM, BLK)
    row = [flat[pl.ds(m, blocks, stride=MOM), :] for m in range(10)]
    for k in range(3):
        pulled = row[k] + row[3 + k] + row[6 + k]
        half = 0.5 * (comp_ref[k * blocks : (k + 1) * blocks, :] * row[9] - pulled)
        hi = half.astype(BF).astype(F32)
        scaled[k * blocks : (k + 1) * blocks, :] = hi
        scaled[(3 + k) * blocks : (4 + k) * blocks, :] = half - hi

    highs = NODE_DEV // BLK
    span = targets * highs
    codes = owner_ref[...]
    place = jnp.zeros_like(codes)
    for code, to in enumerate(codes_to):
        if to:
            place = jnp.where(codes == code, to, place)
    slot = slot_ref[...]
    high = place * highs + (slot >> 7)
    low = slot & 127
    high_at = lax.broadcasted_iota(jnp.int32, (span, BLK), 0)
    low_at = lax.broadcasted_iota(jnp.int32, (BLK, BLK), 0)
    for b in range(blocks):
        lanes = slice(b * BLK, (b + 1) * BLK)
        values = [scaled[m * blocks + b : m * blocks + b + 1, :] for m in range(6)]
        for end in range(2):
            at = slice((2 * b + end) * BLK, (2 * b + end + 1) * BLK)
            hit = high_at == high[end : end + 1, lanes]
            right[:, at] = jnp.where(low_at == low[end : end + 1, lanes], 1.0, 0.0).astype(BF)
            for m in range(6):
                left[m * span : (m + 1) * span, at] = jnp.where(hit, values[m], 0.0).astype(BF)
    summed = lax.dot_general(left[...], right[...], _NT, preferred_element_type=F32)
    total[...] = summed[: 3 * span] + summed[3 * span :]
    for t, out in enumerate(outs):
        for h in range(highs):
            out[:, h * BLK : (h + 1) * BLK] = total[pl.ds(t * highs + h, 3, stride=span), :]


def on_device(segments, node_owner, node_slot, pair_first, pair_second, pair_count):
    width = segments.shape[1]
    blocks = width // BLK
    slots = pair_first.shape[0]
    places = -(-(slots + GROUP) // BLK) * BLK
    peers = lax.axis_size("gz")
    up = [(i, (i + 1) % peers) for i in range(peers)]
    down = [(j, i) for i, j in up]
    below = lax.ppermute(segments, "gz", up)
    above = lax.ppermute(segments, "gz", down)

    listed = jnp.arange(slots, dtype=jnp.int32) < pair_count[0]
    packed = jnp.where(listed, pair_first * 128 + pair_second, -1)

    smem = pl.BlockSpec(memory_space=pltpu.SMEM)
    vmem = pl.BlockSpec(memory_space=pltpu.VMEM)
    params = pltpu.CompilerParams(vmem_limit_bytes=40 << 20)
    table, comp, forces, lists = pl.pallas_call(
        functools.partial(own_kernel, blocks),
        out_shape=(
            jax.ShapeDtypeStruct((blocks, ROWS, 2 * BLK), BF),
            jax.ShapeDtypeStruct((9 * blocks, BLK), F32),
            jax.ShapeDtypeStruct((blocks, MOM, BLK), F32),
            jax.ShapeDtypeStruct((8, places), jnp.int32),
        ),
        in_specs=[vmem, vmem],
        out_specs=(vmem, vmem, vmem, smem),
        scratch_shapes=[
            pltpu.VMEM((ROWS * blocks, BLK), F32),
            pltpu.VMEM((blocks + 1, ROWS, BLK), BF),
            pltpu.VMEM((8, places), jnp.int32),
            pltpu.SemaphoreType.DMA((2,)),
        ],
        compiler_params=params,
        cost_estimate=pl.CostEstimate(flops=10_000_000_000, bytes_accessed=1_000_000, transcendentals=0),
    )(packed, segments)

    columns = lax.axis_size("col")
    stride = columns // 4
    moves = [m % columns for m in (0, 1, -1, stride, -stride)]
    shifts = list(dict.fromkeys(moves))
    targets = len(shifts)
    span = targets * (NODE_DEV // BLK)
    partials = pl.pallas_call(
        functools.partial(halo_kernel, blocks, [shifts.index(m) for m in moves], targets),
        out_shape=tuple(jax.ShapeDtypeStruct((3, NODE_DEV), F32) for _ in shifts),
        in_specs=[smem] + [vmem] * 7,
        out_specs=(vmem,) * targets,
        scratch_shapes=[
            pltpu.VMEM((9 * blocks, BLK), F32),
            pltpu.VMEM((ROWS * blocks, BLK), F32),
            pltpu.VMEM((2 * blocks + 1, ROWS, BLK), BF),
            pltpu.VMEM((blocks, MOM, BLK), F32),
            pltpu.VMEM((6 * blocks, BLK), F32),
            pltpu.VMEM((6 * span, 2 * width), BF),
            pltpu.VMEM((BLK, 2 * width), BF),
            pltpu.VMEM((3 * span, BLK), F32),
        ],
        compiler_params=params,
    )(lists, below, above, table, comp, forces, node_owner, node_slot)
    node_total = partials[0]
    for shift, partial in zip(shifts[1:], partials[1:]):
        node_total = node_total + lax.ppermute(partial, "col", [(i, (i + shift) % columns) for i in range(columns)])
    return node_total


def solution(mesh):
    in_specs = (
        P(None, ("col", "gz")),
        P(None, ("col", "gz")),
        P(None, ("col", "gz")),
        P(("col", "gz")),
        P(("col", "gz")),
        P(("col", "gz")),
    )
    out_specs = P(None, ("col", "gz"))
    return jax.shard_map(
        on_device, mesh=mesh, in_specs=in_specs, out_specs=out_specs, check_vma=False
    )
```

```python
import functools

import jax
import jax.numpy as jnp
from jax import lax
from jax.experimental import pallas as pl
from jax.experimental.pallas import tpu as pltpu
from jax.sharding import PartitionSpec as P

BLK = 128
NODE_DEV = 3072
MU = 0.02
CORE_SQ = 0.5

ROWS = 64
MOM = 16
GROUPS = (128, 64, 32, 16)
WIDE = 256
AHEAD = 16
BF = jnp.bfloat16
F32 = jnp.float32

_TN = (((0,), (0,)), ((), ()))
_NT = (((1,), (1,)), ((), ()))


def split3(v):
    a = v.astype(BF).astype(F32)
    r = v - a
    b = r.astype(BF).astype(F32)
    return a, b, r - b


def gather_components(seg_ref, comp, blocks):
    for b in range(blocks):
        lanes = slice(b * BLK, (b + 1) * BLK)
        comp[pl.ds(b, 8, stride=blocks), :] = seg_ref[0:8, lanes]
        comp[8 * blocks + b : 8 * blocks + b + 1, :] = seg_ref[8:9, lanes]


def features(comp, blocks):
    part = [comp[c * blocks : (c + 1) * blocks, :] for c in range(9)]
    x, burgers, line = part[0:3], part[3:6], part[6:9]
    xs = [split3(v) for v in x]
    norm = x[0] * x[0] + x[1] * x[1] + x[2] * x[2]
    prods = [split3(p * q)[0:1] + (p * q,) for p in burgers for q in line]
    prods = [(hi, full - hi) for hi, full in prods]
    return xs, norm, prods


def source_rows(xs, norm, prods):
    one = jnp.ones_like(norm)
    rows = {}
    norms = split3(norm + CORE_SQ)
    for k in range(3):
        x1, x2, x3 = xs[k]
        rows[k], rows[3 + k], rows[6 + k] = x1, x2, x3
        rows[9 + k], rows[12 + k] = one, norms[k]
        rows[15 + k], rows[18 + k], rows[21 + k] = x1, x2, x1
    for m, (hi, lo) in enumerate(prods):
        rows[32 + m], rows[41 + m], rows[50 + m] = hi, lo, hi
    return rows


def target_rows(xs, norm, prods):
    one = jnp.ones_like(norm)
    rows = {}
    norms = split3(norm)
    for k in range(3):
        x1, x2, x3 = (-2.0 * v for v in xs[k])
        rows[k], rows[3 + k], rows[6 + k] = x1, x1, x1
        rows[9 + k], rows[12 + k] = norms[k], one
        rows[15 + k], rows[18 + k], rows[21 + k] = x2, x2, x3
    for m, (hi, lo) in enumerate(prods):
        rows[32 + m], rows[41 + m], rows[50 + m] = hi, hi, lo
    return rows


def put_rows(rows, feat, blocks):
    for r in range(ROWS):
        feat[r * blocks : (r + 1) * blocks, :] = rows.get(r, jnp.zeros((blocks, BLK), F32))


def block_rows(feat, b, blocks):
    return feat[pl.ds(b, ROWS, stride=blocks), :].astype(BF)


def source_table(comp, feat, table, base, blocks):
    put_rows(source_rows(*features(comp, blocks)), feat, blocks)
    for b in range(blocks):
        table[base + b] = block_rows(feat, b, blocks)


def empty_block(table, at):
    row = lax.broadcasted_iota(jnp.int32, (ROWS, BLK), 0)
    table[at] = jnp.where(row == 12, 1.0, 0.0).astype(BF)


def pair_group(count, start, entry, target, source, forces):
    codes = [entry(start + u) for u in range(count)]

    def products(c):
        return lax.dot_general(source[c & 127], target[c >> 7], _TN, preferred_element_type=F32)

    ahead = {u: products(codes[u]) for u in range(min(AHEAD, count))}
    for u, c in enumerate(codes):
        if u + AHEAD < count:
            ahead[u + AHEAD] = products(codes[u + AHEAD])
        value = ahead.pop(u)
        inverse = lax.rsqrt(value[:, :BLK])
        coupling = value[:, BLK:] * inverse * (inverse * inverse)
        hi = coupling.astype(BF)
        lo = (coupling - hi.astype(F32)).astype(BF)
        moment = source[c & 127, 0:MOM, :]
        moment = jnp.concatenate([moment, moment], axis=1)
        weight = jnp.concatenate([hi, lo], axis=0)
        forces[c >> 7] += jnp.dot(moment, weight, preferred_element_type=F32)


def all_pairs(total, entry, target, source, forces):
    whole = (total + (GROUPS[-1] - 1)) // GROUPS[0]

    def step(q, carry):
        pair_group(GROUPS[0], q * GROUPS[0], entry, target, source, forces)
        return carry

    lax.fori_loop(0, whole, step, 0)
    at = whole * GROUPS[0]
    for count in GROUPS[1:]:
        wanted = total > at + (count - GROUPS[-1] if count > GROUPS[-1] else 0)

        @pl.when(wanted)
        def _(count=count, at=at):
            pair_group(count, at, entry, target, source, forces)

        at = at + jnp.where(wanted, count, 0)


def sort_pairs(blocks, packed, lists):
    slots, places = packed.shape[1], lists.shape[1]
    listed = packed >= 0
    first, second = packed >> 7, packed & 127
    near = jnp.where(jnp.logical_and(listed, second < 2 * blocks), 1.0, 0.0)
    far = jnp.where(listed, 1.0, 0.0) - near
    line = lax.broadcasted_iota(jnp.int32, (16, slots), 0)
    member = jnp.where(line == 0, near, jnp.where(line == 1, far, 0.0)).astype(BF)
    before = lax.broadcasted_iota(jnp.int32, (slots, slots), 0) < lax.broadcasted_iota(jnp.int32, (slots, slots), 1)
    rank = jnp.dot(member, jnp.where(before, 1.0, 0.0).astype(BF), preferred_element_type=F32)
    source = second - jnp.where(second >= 2 * blocks, 2 * blocks, 0)
    value = jnp.where(line == 0, first, jnp.where(line == 1, source, 0)).astype(F32).astype(BF)
    place = lax.broadcasted_iota(jnp.int32, (places, slots), 0).astype(F32)
    for r, (mine, empty) in enumerate(((near, 2 * blocks), (far, blocks))):
        at = jnp.where(mine > 0.0, rank[r : r + 1], -1.0)
        hit = jnp.where(place == at, 1.0, 0.0).astype(BF)
        found = lax.dot_general(value, hit, _NT, preferred_element_type=F32)
        code = (found[0:1] * 128.0 + found[1:2]).astype(jnp.int32)
        total = jnp.sum(mine, axis=1, keepdims=True).astype(jnp.int32)
        lane = lax.broadcasted_iota(jnp.int32, (1, places), 1)
        lists[r : r + 1, :] = jnp.where(lane < total, code, empty)
        lists[2 + r : 3 + r, :] = jnp.broadcast_to(total, (1, places))


def near_kernel(
    blocks, packed_ref, seg_ref, near_ref,
    forces_ref, target_ref, comp_ref, lists_ref,
    comp, feat, source, lists, done,
):
    sort_pairs(blocks, packed_ref[...].reshape(1, packed_ref.shape[0]), lists)
    copy = pltpu.make_async_copy(lists, lists_ref, done)
    copy.start()
    gather_components(near_ref, comp, blocks)
    source_table(comp, feat, source, blocks, blocks)
    empty_block(source, 2 * blocks)
    gather_components(seg_ref, comp_ref, blocks)
    parts = features(comp_ref, blocks)
    put_rows(source_rows(*parts), feat, blocks)
    for b in range(blocks):
        source[b] = block_rows(feat, b, blocks)
    xs, norm, prods = parts
    part = [comp_ref[c * blocks : (c + 1) * blocks, :] for c in range(3, 9)]
    scaled = [MU * p * q for p in part[0:3] for q in part[3:6]]
    scaled = [(split3(v)[0], v) for v in scaled]
    scaled = [(hi, full - hi) for hi, full in scaled]
    put_rows(target_rows(xs, norm, scaled), feat, blocks)
    blank = jnp.zeros((ROWS // 2, BLK), BF)
    for b in range(blocks):
        rows = block_rows(feat, b, blocks)
        target_ref[b, 0:32, 0:BLK] = rows[0:32]
        target_ref[b, 0:32, BLK:] = blank
        target_ref[b, 32:64, 0:BLK] = blank
        target_ref[b, 32:64, BLK:] = rows[32:64]
    forces_ref[...] = jnp.zeros_like(forces_ref)
    copy.wait()
    all_pairs(lists_ref[2, 0], lambda p: lists_ref[0, p], target_ref, source, forces_ref)


def one_hot(at, row):
    return jnp.where(at == row, jnp.ones((), BF), jnp.zeros((), BF))


def span_of(targets):
    return -(-targets * (NODE_DEV // WIDE) // 8) * 8


def far_kernel(
    blocks, steps, lists_ref, far_ref, target_ref, comp_ref, near_forces,
    owner_ref, slot_ref, *rest,
):
    targets = 1 + 2 * len(set(steps))
    outs, (comp, feat, source, forces, scaled, total_low, total_high) = rest[:targets], rest[targets:]
    gather_components(far_ref, comp, blocks)
    source_table(comp, feat, source, 0, blocks)
    empty_block(source, blocks)
    forces[...] = near_forces[...]
    all_pairs(lists_ref[3, 0], lambda p: lists_ref[1, p], target_ref, source, forces)

    flat = forces.reshape(blocks * MOM, BLK)
    row = [flat[pl.ds(m, blocks, stride=MOM), :] for m in range(10)]
    for k in range(3):
        pulled = row[k] + row[3 + k] + row[6 + k]
        half = 0.5 * (comp_ref[k * blocks : (k + 1) * blocks, :] * row[9] - pulled)
        hi = half.astype(BF).astype(F32)
        scaled[k * blocks : (k + 1) * blocks, :] = hi
        scaled[(3 + k) * blocks : (4 + k) * blocks, :] = half - hi

    highs = NODE_DEV // WIDE
    span = span_of(targets)
    codes = owner_ref[...]
    column = lax.axis_index("col")
    place = jnp.zeros_like(codes)
    for n, step in enumerate(steps):
        to = 1 + 2 * steps.index(step)
        odd = (column // step) % 2
        place = jnp.where(codes == 1 + 2 * n, to + odd, place)
        place = jnp.where(codes == 2 + 2 * n, to + 1 - odd, place)
    slot = slot_ref[...]
    high = place * highs + slot // WIDE
    low = slot % WIDE
    high, low = high.astype(F32).astype(BF), low.astype(F32).astype(BF)
    high_at = lax.broadcasted_iota(jnp.int32, (span, BLK), 0).astype(F32).astype(BF)
    low_at = lax.broadcasted_iota(jnp.int32, (WIDE, BLK), 0).astype(F32).astype(BF)
    summed = None
    for first in range(0, blocks, 4):
        lefts, rights = [], []
        for b in range(first, first + 4):
            lanes = slice(b * BLK, (b + 1) * BLK)
            values = [scaled[m * blocks + b : m * blocks + b + 1, :].astype(BF) for m in range(6)]
            for end in range(2):
                rights.append(one_hot(low_at, low[end : end + 1, lanes]))
                hit = one_hot(high_at, high[end : end + 1, lanes])
                lefts.append(jnp.concatenate([hit * value for value in values], axis=0))
        part = lax.dot_general(
            jnp.concatenate(lefts, axis=1), jnp.concatenate(rights, axis=1), _NT, preferred_element_type=F32
        )
        summed = part if summed is None else summed + part
    summed = summed[: 3 * span] + summed[3 * span :]
    for half, total in enumerate((total_low, total_high)):
        total[...] = summed[:, half * BLK : (half + 1) * BLK]
    for t, out in enumerate(outs):
        for h in range(highs):
            for half, total in enumerate((total_low, total_high)):
                out[:, h * WIDE + half * BLK : h * WIDE + (half + 1) * BLK] = total[pl.ds(t * highs + h, 3, stride=span), :]


def swaps(peers, step, late):
    firsts = [i for i in range(peers) if (i // step) % 2 == late]
    return [(i, (i + step) % peers) for i in firsts] + [((i + step) % peers, i) for i in firsts]


def on_device(segments, node_owner, node_slot, pair_first, pair_second, pair_count):
    width = segments.shape[1]
    blocks = width // BLK
    slots = pair_first.shape[0]
    places = -(-(slots + GROUPS[0]) // BLK) * BLK
    peers = lax.axis_size("gz")
    smem = pl.BlockSpec(memory_space=pltpu.SMEM)
    vmem = pl.BlockSpec(memory_space=pltpu.VMEM)
    params = pltpu.CompilerParams(vmem_limit_bytes=40 << 20)

    near = lax.ppermute(segments, "gz", swaps(peers, 1, 0))
    far = lax.ppermute(segments, "gz", swaps(peers, 1, 1))

    odd = lax.axis_index("gz") % 2
    beyond = jnp.where(odd == 1, pair_second < blocks, pair_second >= 2 * blocks)
    own = jnp.logical_and(pair_second >= blocks, pair_second < 2 * blocks)
    region = jnp.where(own, 0, jnp.where(beyond, 1, 2))
    old = jnp.where(pair_second >= 2 * blocks, 2, jnp.where(pair_second >= blocks, 1, 0))
    renumbered = pair_second + (region - old) * blocks
    listed = jnp.arange(slots, dtype=jnp.int32) < pair_count[0]
    packed = jnp.where(listed, pair_first * 128 + renumbered, -1)

    forces, table, comp, lists = pl.pallas_call(
        functools.partial(near_kernel, blocks),
        out_shape=(
            jax.ShapeDtypeStruct((blocks, MOM, BLK), F32),
            jax.ShapeDtypeStruct((blocks, ROWS, 2 * BLK), BF),
            jax.ShapeDtypeStruct((9 * blocks, BLK), F32),
            jax.ShapeDtypeStruct((8, places), jnp.int32),
        ),
        in_specs=[vmem, vmem, vmem],
        out_specs=(vmem, vmem, vmem, smem),
        scratch_shapes=[
            pltpu.VMEM((9 * blocks, BLK), F32),
            pltpu.VMEM((ROWS * blocks, BLK), F32),
            pltpu.VMEM((2 * blocks + 1, ROWS, BLK), BF),
            pltpu.VMEM((8, places), jnp.int32),
            pltpu.SemaphoreType.DMA,
        ],
        compiler_params=params,
        cost_estimate=pl.CostEstimate(flops=10_000_000_000, bytes_accessed=1_000_000, transcendentals=0),
    )(packed, segments, near)

    columns = lax.axis_size("col")
    steps = (1, columns // 4)
    distinct = list(dict.fromkeys(steps))
    targets = 1 + 2 * len(distinct)
    span = span_of(targets)
    partials = pl.pallas_call(
        functools.partial(far_kernel, blocks, steps),
        out_shape=tuple(jax.ShapeDtypeStruct((3, NODE_DEV), F32) for _ in range(targets)),
        in_specs=[smem] + [vmem] * 6,
        out_specs=(vmem,) * targets,
        scratch_shapes=[
            pltpu.VMEM((9 * blocks, BLK), F32),
            pltpu.VMEM((ROWS * blocks, BLK), F32),
            pltpu.VMEM((blocks + 1, ROWS, BLK), BF),
            pltpu.VMEM((blocks, MOM, BLK), F32),
            pltpu.VMEM((6 * blocks, BLK), F32),
            pltpu.VMEM((3 * span, BLK), F32),
            pltpu.VMEM((3 * span, BLK), F32),
        ],
        compiler_params=params,
    )(lists, far, table, comp, forces, node_owner, node_slot)
    node_total = partials[0]
    for n, partial in enumerate(partials[1:]):
        node_total = node_total + lax.ppermute(partial, "col", swaps(columns, distinct[n // 2], n % 2))
    return node_total


def solution(mesh):
    in_specs = (
        P(None, ("col", "gz")),
        P(None, ("col", "gz")),
        P(None, ("col", "gz")),
        P(("col", "gz")),
        P(("col", "gz")),
        P(("col", "gz")),
    )
    out_specs = P(None, ("col", "gz"))
    return jax.shard_map(
        on_device, mesh=mesh, in_specs=in_specs, out_specs=out_specs, check_vma=False
    )
```

```python
import functools

import jax
import jax.numpy as jnp
from jax import lax
from jax.experimental import pallas as pl
from jax.experimental.pallas import tpu as pltpu
from jax.sharding import PartitionSpec as P

BLK = 128
NODE_DEV = 3072
MU = 0.02
CORE_SQ = 0.5

ROWS = 64
MOM = 16
GROUPS = (128, 64, 32, 16)
WIDE = 256
EARLY = 64
AHEAD = 16
BF = jnp.bfloat16
F32 = jnp.float32

_TN = (((0,), (0,)), ((), ()))
_NT = (((1,), (1,)), ((), ()))


def split3(v):
    a = v.astype(BF).astype(F32)
    r = v - a
    b = r.astype(BF).astype(F32)
    return a, b, r - b


def gather_components(seg_ref, comp, blocks):
    for b in range(blocks):
        lanes = slice(b * BLK, (b + 1) * BLK)
        comp[pl.ds(b, 8, stride=blocks), :] = seg_ref[0:8, lanes]
        comp[8 * blocks + b : 8 * blocks + b + 1, :] = seg_ref[8:9, lanes]


def features(comp, blocks):
    part = [comp[c * blocks : (c + 1) * blocks, :] for c in range(9)]
    x, burgers, line = part[0:3], part[3:6], part[6:9]
    xs = [split3(v) for v in x]
    norm = x[0] * x[0] + x[1] * x[1] + x[2] * x[2]
    prods = [split3(p * q)[0:1] + (p * q,) for p in burgers for q in line]
    prods = [(hi, full - hi) for hi, full in prods]
    return xs, norm, prods


def source_rows(xs, norm, prods):
    one = jnp.ones_like(norm)
    rows = {}
    norms = split3(norm + CORE_SQ)
    for k in range(3):
        x1, x2, x3 = xs[k]
        rows[k], rows[3 + k], rows[6 + k] = x1, x2, x3
        rows[9 + k], rows[12 + k] = one, norms[k]
        rows[15 + k], rows[18 + k], rows[21 + k] = x1, x2, x1
    for m, (hi, lo) in enumerate(prods):
        rows[32 + m], rows[41 + m], rows[50 + m] = hi, lo, hi
    return rows


def target_rows(xs, norm, prods):
    one = jnp.ones_like(norm)
    rows = {}
    norms = split3(norm)
    for k in range(3):
        x1, x2, x3 = (-2.0 * v for v in xs[k])
        rows[k], rows[3 + k], rows[6 + k] = x1, x1, x1
        rows[9 + k], rows[12 + k] = norms[k], one
        rows[15 + k], rows[18 + k], rows[21 + k] = x2, x2, x3
    for m, (hi, lo) in enumerate(prods):
        rows[32 + m], rows[41 + m], rows[50 + m] = hi, hi, lo
    return rows


def put_rows(rows, feat, blocks):
    for r in range(ROWS):
        feat[r * blocks : (r + 1) * blocks, :] = rows.get(r, jnp.zeros((blocks, BLK), F32))


def block_rows(feat, b, blocks):
    return feat[pl.ds(b, ROWS, stride=blocks), :].astype(BF)


def source_table(comp, feat, table, base, blocks):
    put_rows(source_rows(*features(comp, blocks)), feat, blocks)
    for b in range(blocks):
        table[base + b] = block_rows(feat, b, blocks)


def empty_block(table, at):
    row = lax.broadcasted_iota(jnp.int32, (ROWS, BLK), 0)
    table[at] = jnp.where(row == 12, 1.0, 0.0).astype(BF)


def pair_group(count, start, entry, target, source, forces):
    codes = [entry(start + u) for u in range(count)]

    def products(c):
        return lax.dot_general(source[c & 127], target[c >> 7], _TN, preferred_element_type=F32)

    ahead = {u: products(codes[u]) for u in range(min(AHEAD, count))}
    for u, c in enumerate(codes):
        if u + AHEAD < count:
            ahead[u + AHEAD] = products(codes[u + AHEAD])
        value = ahead.pop(u)
        inverse = lax.rsqrt(value[:, :BLK])
        coupling = value[:, BLK:] * inverse * (inverse * inverse)
        hi = coupling.astype(BF)
        lo = (coupling - hi.astype(F32)).astype(BF)
        moment = source[c & 127, 0:MOM, :]
        moment = jnp.concatenate([moment, moment], axis=1)
        weight = jnp.concatenate([hi, lo], axis=0)
        forces[c >> 7] += jnp.dot(moment, weight, preferred_element_type=F32)


def all_pairs(total, entry, target, source, forces, groups=GROUPS):
    whole = (total + (groups[-1] - 1)) // groups[0]

    def step(q, carry):
        pair_group(groups[0], q * groups[0], entry, target, source, forces)
        return carry

    lax.fori_loop(0, whole, step, 0)
    at = whole * groups[0]
    for count in groups[1:]:
        wanted = total > at + (count - groups[-1] if count > groups[-1] else 0)

        @pl.when(wanted)
        def _(count=count, at=at):
            pair_group(count, at, entry, target, source, forces)

        at = at + jnp.where(wanted, count, 0)


def sort_pairs(blocks, packed, lists):
    slots, places = packed.shape[1], lists.shape[1]
    listed = packed >= 0
    first, second = packed >> 7, packed & 127
    own = jnp.where(jnp.logical_and(listed, second < blocks), 1.0, 0.0)
    near = jnp.where(jnp.logical_and(listed, second < 2 * blocks), 1.0, 0.0)
    far = jnp.where(listed, 1.0, 0.0) - near
    line = lax.broadcasted_iota(jnp.int32, (16, slots), 0)
    member = jnp.where(line == 0, near - own, jnp.where(line == 1, far, jnp.where(line == 2, own, 0.0))).astype(BF)
    before = lax.broadcasted_iota(jnp.int32, (slots, slots), 0) < lax.broadcasted_iota(jnp.int32, (slots, slots), 1)
    rank = jnp.dot(member, jnp.where(before, 1.0, 0.0).astype(BF), preferred_element_type=F32)
    source = second - jnp.where(second >= 2 * blocks, 2 * blocks, 0)
    value = jnp.where(line == 0, first, jnp.where(line == 1, source, 0)).astype(F32).astype(BF)
    place = lax.broadcasted_iota(jnp.int32, (places, slots), 0).astype(F32)
    owned = jnp.sum(own, axis=1, keepdims=True)
    first_rank = jnp.where(own > 0.0, rank[2:3], rank[0:1] + owned)
    for r, (mine, ranks, empty) in enumerate(((near, first_rank, 2 * blocks), (far, rank[1:2], blocks))):
        at = jnp.where(mine > 0.0, ranks, -1.0)
        hit = jnp.where(place == at, 1.0, 0.0).astype(BF)
        found = lax.dot_general(value, hit, _NT, preferred_element_type=F32)
        code = (found[0:1] * 128.0 + found[1:2]).astype(jnp.int32)
        total = jnp.sum(mine, axis=1, keepdims=True).astype(jnp.int32)
        lane = lax.broadcasted_iota(jnp.int32, (1, places), 1)
        lists[r : r + 1, :] = jnp.where(lane < total, code, empty)
        lists[2 + r : 3 + r, :] = jnp.broadcast_to(total, (1, places))
    lists[4:5, :] = jnp.broadcast_to(owned.astype(jnp.int32), (1, places))


def own_tables(blocks, comp, feat, source, target):
    parts = features(comp, blocks)
    put_rows(source_rows(*parts), feat, blocks)
    for b in range(blocks):
        source[b] = block_rows(feat, b, blocks)
    xs, norm, prods = parts
    part = [comp[c * blocks : (c + 1) * blocks, :] for c in range(3, 9)]
    scaled = [MU * p * q for p in part[0:3] for q in part[3:6]]
    scaled = [(split3(v)[0], v) for v in scaled]
    scaled = [(hi, full - hi) for hi, full in scaled]
    put_rows(target_rows(xs, norm, scaled), feat, blocks)
    blank = jnp.zeros((ROWS // 2, BLK), BF)
    for b in range(blocks):
        rows = block_rows(feat, b, blocks)
        target[b, 0:32, 0:BLK] = rows[0:32]
        target[b, 0:32, BLK:] = blank
        target[b, 32:64, 0:BLK] = blank
        target[b, 32:64, BLK:] = rows[32:64]


def early_pairs(lists_ref):
    return jnp.minimum(lists_ref[4, 0] // GROUPS[-1] * GROUPS[-1], EARLY)


def first_kernel(
    blocks, packed_ref, seg_ref,
    lists, forces, source, target, comp,
    feat, counted, done,
):
    gather_components(seg_ref, comp, blocks)

    @pl.when(lax.axis_index("gz") == 0)
    def _():
        sort_pairs(blocks, packed_ref[...].reshape(1, packed_ref.shape[0]), lists)
        copy = pltpu.make_async_copy(lists, counted, done)
        copy.start()
        own_tables(blocks, comp, feat, source, target)
        forces[...] = jnp.zeros_like(forces)
        copy.wait()
        all_pairs(early_pairs(counted), lambda p: counted[0, p], target, source, forces, GROUPS[1:])


def near_kernel(
    blocks, packed_ref, near_ref, own_comp, early_lists, early_forces, early_source, early_target,
    forces_ref, target_ref, lists_ref,
    comp, feat, source, lists, done,
):
    early = lax.axis_index("gz") == 0
    copy = pltpu.make_async_copy(lists, lists_ref, done)

    @pl.when(early)
    def _():
        lists[...] = early_lists[...]
        copy.start()
        forces_ref[...] = early_forces[...]
        target_ref[...] = early_target[...]
        source[0:blocks] = early_source[...]

    @pl.when(jnp.logical_not(early))
    def _():
        sort_pairs(blocks, packed_ref[...].reshape(1, packed_ref.shape[0]), lists)
        copy.start()
        own_tables(blocks, own_comp, feat, source, target_ref)
        forces_ref[...] = jnp.zeros_like(forces_ref)

    gather_components(near_ref, comp, blocks)
    source_table(comp, feat, source, blocks, blocks)
    empty_block(source, 2 * blocks)
    copy.wait()
    base = jnp.where(early, early_pairs(lists_ref), 0)
    all_pairs(lists_ref[2, 0] - base, lambda p: lists_ref[0, base + p], target_ref, source, forces_ref)


def one_hot(at, row):
    return jnp.where(at == row, jnp.ones((), BF), jnp.zeros((), BF))


def span_of(targets):
    return -(-targets * (NODE_DEV // WIDE) // 8) * 8


def far_kernel(
    blocks, steps, lists_ref, far_ref, target_ref, comp_ref, near_forces,
    owner_ref, slot_ref, *rest,
):
    targets = 1 + 2 * len(set(steps))
    outs, (feat, source, forces, scaled, total_low, total_high) = rest[:targets], rest[targets:]
    source_table(far_ref, feat, source, 0, blocks)
    empty_block(source, blocks)
    forces[...] = near_forces[...]
    all_pairs(lists_ref[3, 0], lambda p: lists_ref[1, p], target_ref, source, forces)

    flat = forces.reshape(blocks * MOM, BLK)
    row = [flat[pl.ds(m, blocks, stride=MOM), :] for m in range(10)]
    for k in range(3):
        pulled = row[k] + row[3 + k] + row[6 + k]
        half = 0.5 * (comp_ref[k * blocks : (k + 1) * blocks, :] * row[9] - pulled)
        hi = half.astype(BF).astype(F32)
        scaled[k * blocks : (k + 1) * blocks, :] = hi
        scaled[(3 + k) * blocks : (4 + k) * blocks, :] = half - hi

    highs = NODE_DEV // WIDE
    span = span_of(targets)
    codes = owner_ref[...]
    column = lax.axis_index("col")
    place = jnp.zeros_like(codes)
    for n, step in enumerate(steps):
        to = 1 + 2 * steps.index(step)
        odd = (column // step) % 2
        place = jnp.where(codes == 1 + 2 * n, to + odd, place)
        place = jnp.where(codes == 2 + 2 * n, to + 1 - odd, place)
    slot = slot_ref[...]
    high = place * highs + slot // WIDE
    low = slot % WIDE
    high, low = high.astype(F32).astype(BF), low.astype(F32).astype(BF)
    high_at = lax.broadcasted_iota(jnp.int32, (span, BLK), 0).astype(F32).astype(BF)
    low_at = lax.broadcasted_iota(jnp.int32, (WIDE, BLK), 0).astype(F32).astype(BF)
    summed = None
    for first in range(0, blocks, 4):
        lefts, rights = [], []
        for b in range(first, first + 4):
            lanes = slice(b * BLK, (b + 1) * BLK)
            values = [scaled[m * blocks + b : m * blocks + b + 1, :].astype(BF) for m in range(6)]
            for end in range(2):
                rights.append(one_hot(low_at, low[end : end + 1, lanes]))
                hit = one_hot(high_at, high[end : end + 1, lanes])
                lefts.append(jnp.concatenate([hit * value for value in values], axis=0))
        part = lax.dot_general(
            jnp.concatenate(lefts, axis=1), jnp.concatenate(rights, axis=1), _NT, preferred_element_type=F32
        )
        summed = part if summed is None else summed + part
    summed = summed[: 3 * span] + summed[3 * span :]
    for half, total in enumerate((total_low, total_high)):
        total[...] = summed[:, half * BLK : (half + 1) * BLK]
    for t, out in enumerate(outs):
        for h in range(highs):
            for half, total in enumerate((total_low, total_high)):
                out[:, h * WIDE + half * BLK : h * WIDE + (half + 1) * BLK] = total[pl.ds(t * highs + h, 3, stride=span), :]


def swaps(peers, step, late):
    firsts = [i for i in range(peers) if (i // step) % 2 == late]
    return [(i, (i + step) % peers) for i in firsts] + [((i + step) % peers, i) for i in firsts]


def on_device(segments, node_owner, node_slot, pair_first, pair_second, pair_count):
    width = segments.shape[1]
    blocks = width // BLK
    slots = pair_first.shape[0]
    places = -(-(slots + GROUPS[0]) // BLK) * BLK
    peers = lax.axis_size("gz")
    smem = pl.BlockSpec(memory_space=pltpu.SMEM)
    vmem = pl.BlockSpec(memory_space=pltpu.VMEM)
    params = pltpu.CompilerParams(vmem_limit_bytes=40 << 20)

    near = lax.ppermute(segments, "gz", swaps(peers, 1, 0))

    odd = lax.axis_index("gz") % 2
    beyond = jnp.where(odd == 1, pair_second < blocks, pair_second >= 2 * blocks)
    own = jnp.logical_and(pair_second >= blocks, pair_second < 2 * blocks)
    region = jnp.where(own, 0, jnp.where(beyond, 1, 2))
    old = jnp.where(pair_second >= 2 * blocks, 2, jnp.where(pair_second >= blocks, 1, 0))
    renumbered = pair_second + (region - old) * blocks
    listed = jnp.arange(slots, dtype=jnp.int32) < pair_count[0]
    packed = jnp.where(listed, pair_first * 128 + renumbered, -1)

    early_shapes = (
        jax.ShapeDtypeStruct((8, places), jnp.int32),
        jax.ShapeDtypeStruct((blocks, MOM, BLK), F32),
        jax.ShapeDtypeStruct((blocks, ROWS, BLK), BF),
        jax.ShapeDtypeStruct((blocks, ROWS, 2 * BLK), BF),
        jax.ShapeDtypeStruct((9 * blocks, BLK), F32),
    )
    early = pl.pallas_call(
        functools.partial(first_kernel, blocks),
        out_shape=early_shapes,
        in_specs=[vmem, vmem],
        out_specs=(vmem,) * 5,
        scratch_shapes=[
            pltpu.VMEM((ROWS * blocks, BLK), F32),
            pltpu.SMEM((8, places), jnp.int32),
            pltpu.SemaphoreType.DMA,
        ],
        compiler_params=params,
    )(packed, segments)
    *early, comp = early
    far = lax.ppermute(comp, "gz", swaps(peers, 1, 1))

    forces, table, lists = pl.pallas_call(
        functools.partial(near_kernel, blocks),
        out_shape=(
            jax.ShapeDtypeStruct((blocks, MOM, BLK), F32),
            jax.ShapeDtypeStruct((blocks, ROWS, 2 * BLK), BF),
            jax.ShapeDtypeStruct((8, places), jnp.int32),
        ),
        in_specs=[vmem] * 7,
        out_specs=(vmem, vmem, smem),
        scratch_shapes=[
            pltpu.VMEM((9 * blocks, BLK), F32),
            pltpu.VMEM((ROWS * blocks, BLK), F32),
            pltpu.VMEM((2 * blocks + 1, ROWS, BLK), BF),
            pltpu.VMEM((8, places), jnp.int32),
            pltpu.SemaphoreType.DMA,
        ],
        compiler_params=params,
        cost_estimate=pl.CostEstimate(flops=10_000_000_000, bytes_accessed=1_000_000, transcendentals=0),
    )(packed, near, comp, *early)

    columns = lax.axis_size("col")
    steps = (1, columns // 4)
    distinct = list(dict.fromkeys(steps))
    targets = 1 + 2 * len(distinct)
    span = span_of(targets)
    partials = pl.pallas_call(
        functools.partial(far_kernel, blocks, steps),
        out_shape=tuple(jax.ShapeDtypeStruct((3, NODE_DEV), F32) for _ in range(targets)),
        in_specs=[smem] + [vmem] * 6,
        out_specs=(vmem,) * targets,
        scratch_shapes=[
            pltpu.VMEM((ROWS * blocks, BLK), F32),
            pltpu.VMEM((blocks + 1, ROWS, BLK), BF),
            pltpu.VMEM((blocks, MOM, BLK), F32),
            pltpu.VMEM((6 * blocks, BLK), F32),
            pltpu.VMEM((3 * span, BLK), F32),
            pltpu.VMEM((3 * span, BLK), F32),
        ],
        compiler_params=params,
    )(lists, far, table, comp, forces, node_owner, node_slot)
    node_total = partials[0]
    for n, partial in enumerate(partials[1:]):
        node_total = node_total + lax.ppermute(partial, "col", swaps(columns, distinct[n // 2], n % 2))
    return node_total


def solution(mesh):
    in_specs = (
        P(None, ("col", "gz")),
        P(None, ("col", "gz")),
        P(None, ("col", "gz")),
        P(("col", "gz")),
        P(("col", "gz")),
        P(("col", "gz")),
    )
    out_specs = P(None, ("col", "gz"))
    return jax.shard_map(
        on_device, mesh=mesh, in_specs=in_specs, out_specs=out_specs, check_vma=False
    )
```

```python
import functools

import jax
import jax.numpy as jnp
from jax import lax
from jax.experimental import pallas as pl
from jax.experimental.pallas import tpu as pltpu
from jax.sharding import PartitionSpec as P

BLK = 128
NODE_DEV = 3072
MU = 0.02
CORE_SQ = 0.5

ROWS = 64
MOM = 16
GROUPS = (128, 64, 32, 16)
WIDE = 256
EARLY = 32
AHEAD = 16
BF = jnp.bfloat16
F32 = jnp.float32

_TN = (((0,), (0,)), ((), ()))
_NT = (((1,), (1,)), ((), ()))


def split3(v):
    a = v.astype(BF).astype(F32)
    r = v - a
    b = r.astype(BF).astype(F32)
    return a, b, r - b


def gather_components(seg_ref, comp, blocks):
    for b in range(blocks):
        lanes = slice(b * BLK, (b + 1) * BLK)
        comp[pl.ds(b, 8, stride=blocks), :] = seg_ref[0:8, lanes]
        comp[8 * blocks + b : 8 * blocks + b + 1, :] = seg_ref[8:9, lanes]


def features(comp, blocks):
    part = [comp[c * blocks : (c + 1) * blocks, :] for c in range(9)]
    x, burgers, line = part[0:3], part[3:6], part[6:9]
    xs = [split3(v) for v in x]
    norm = x[0] * x[0] + x[1] * x[1] + x[2] * x[2]
    prods = [split3(p * q)[0:1] + (p * q,) for p in burgers for q in line]
    prods = [(hi, full - hi) for hi, full in prods]
    return xs, norm, prods


def source_rows(xs, norm, prods):
    one = jnp.ones_like(norm)
    rows = {}
    norms = split3(norm + CORE_SQ)
    for k in range(3):
        x1, x2, x3 = xs[k]
        rows[k], rows[3 + k], rows[6 + k] = x1, x2, x3
        rows[9 + k], rows[12 + k] = one, norms[k]
        rows[15 + k], rows[18 + k], rows[21 + k] = x1, x2, x1
    for m, (hi, lo) in enumerate(prods):
        rows[32 + m], rows[41 + m], rows[50 + m] = hi, lo, hi
    return rows


def target_rows(xs, norm, prods):
    one = jnp.ones_like(norm)
    rows = {}
    norms = split3(norm)
    for k in range(3):
        x1, x2, x3 = (-2.0 * v for v in xs[k])
        rows[k], rows[3 + k], rows[6 + k] = x1, x1, x1
        rows[9 + k], rows[12 + k] = norms[k], one
        rows[15 + k], rows[18 + k], rows[21 + k] = x2, x2, x3
    for m, (hi, lo) in enumerate(prods):
        rows[32 + m], rows[41 + m], rows[50 + m] = hi, hi, lo
    return rows


def put_rows(rows, feat, blocks):
    for r in range(ROWS):
        feat[r * blocks : (r + 1) * blocks, :] = rows.get(r, jnp.zeros((blocks, BLK), F32))


def block_rows(feat, b, blocks):
    return feat[pl.ds(b, ROWS, stride=blocks), :].astype(BF)


def source_table(comp, feat, table, base, blocks):
    put_rows(source_rows(*features(comp, blocks)), feat, blocks)
    for b in range(blocks):
        table[base + b] = block_rows(feat, b, blocks)


def empty_block(table, at):
    row = lax.broadcasted_iota(jnp.int32, (ROWS, BLK), 0)
    table[at] = jnp.where(row == 12, 1.0, 0.0).astype(BF)


def pair_group(count, start, entry, target, source, forces):
    codes = [entry(start + u) for u in range(count)]

    def products(c):
        return lax.dot_general(source[c & 127], target[c >> 7], _TN, preferred_element_type=F32)

    ahead = {u: products(codes[u]) for u in range(min(AHEAD, count))}
    for u, c in enumerate(codes):
        if u + AHEAD < count:
            ahead[u + AHEAD] = products(codes[u + AHEAD])
        value = ahead.pop(u)
        inverse = lax.rsqrt(value[:, :BLK])
        coupling = value[:, BLK:] * inverse * (inverse * inverse)
        hi = coupling.astype(BF)
        lo = (coupling - hi.astype(F32)).astype(BF)
        moment = source[c & 127, 0:MOM, :]
        moment = jnp.concatenate([moment, moment], axis=1)
        weight = jnp.concatenate([hi, lo], axis=0)
        forces[c >> 7] += jnp.dot(moment, weight, preferred_element_type=F32)


def all_pairs(total, entry, target, source, forces, groups=GROUPS):
    whole = (total + (groups[-1] - 1)) // groups[0]

    def step(q, carry):
        pair_group(groups[0], q * groups[0], entry, target, source, forces)
        return carry

    lax.fori_loop(0, whole, step, 0)
    at = whole * groups[0]
    for count in groups[1:]:
        wanted = total > at + (count - groups[-1] if count > groups[-1] else 0)

        @pl.when(wanted)
        def _(count=count, at=at):
            pair_group(count, at, entry, target, source, forces)

        at = at + jnp.where(wanted, count, 0)


def sort_pairs(blocks, packed, lists):
    slots, places = packed.shape[1], lists.shape[1]
    listed = packed >= 0
    first, second = packed >> 7, packed & 127
    own = jnp.where(jnp.logical_and(listed, second < blocks), 1.0, 0.0)
    near = jnp.where(jnp.logical_and(listed, second < 2 * blocks), 1.0, 0.0)
    far = jnp.where(listed, 1.0, 0.0) - near
    line = lax.broadcasted_iota(jnp.int32, (16, slots), 0)
    member = jnp.where(line == 0, near - own, jnp.where(line == 1, far, jnp.where(line == 2, own, 0.0))).astype(BF)
    before = lax.broadcasted_iota(jnp.int32, (slots, slots), 0) < lax.broadcasted_iota(jnp.int32, (slots, slots), 1)
    rank = jnp.dot(member, jnp.where(before, 1.0, 0.0).astype(BF), preferred_element_type=F32)
    source = second - jnp.where(second >= 2 * blocks, 2 * blocks, 0)
    value = jnp.where(line == 0, first, jnp.where(line == 1, source, 0)).astype(F32).astype(BF)
    place = lax.broadcasted_iota(jnp.int32, (places, slots), 0).astype(F32)
    owned = jnp.sum(own, axis=1, keepdims=True)
    first_rank = jnp.where(own > 0.0, rank[2:3], rank[0:1] + owned)
    for r, (mine, ranks, empty) in enumerate(((near, first_rank, 2 * blocks), (far, rank[1:2], blocks))):
        at = jnp.where(mine > 0.0, ranks, -1.0)
        hit = jnp.where(place == at, 1.0, 0.0).astype(BF)
        found = lax.dot_general(value, hit, _NT, preferred_element_type=F32)
        code = (found[0:1] * 128.0 + found[1:2]).astype(jnp.int32)
        total = jnp.sum(mine, axis=1, keepdims=True).astype(jnp.int32)
        lane = lax.broadcasted_iota(jnp.int32, (1, places), 1)
        lists[r : r + 1, :] = jnp.where(lane < total, code, empty)
        lists[2 + r : 3 + r, :] = jnp.broadcast_to(total, (1, places))
    lists[4:5, :] = jnp.broadcast_to(owned.astype(jnp.int32), (1, places))


def own_tables(blocks, comp, feat, source, target):
    parts = features(comp, blocks)
    put_rows(source_rows(*parts), feat, blocks)
    for b in range(blocks):
        source[b] = block_rows(feat, b, blocks)
    xs, norm, prods = parts
    part = [comp[c * blocks : (c + 1) * blocks, :] for c in range(3, 9)]
    scaled = [MU * p * q for p in part[0:3] for q in part[3:6]]
    scaled = [(split3(v)[0], v) for v in scaled]
    scaled = [(hi, full - hi) for hi, full in scaled]
    put_rows(target_rows(xs, norm, scaled), feat, blocks)
    blank = jnp.zeros((ROWS // 2, BLK), BF)
    for b in range(blocks):
        rows = block_rows(feat, b, blocks)
        target[b, 0:32, 0:BLK] = rows[0:32]
        target[b, 0:32, BLK:] = blank
        target[b, 32:64, 0:BLK] = blank
        target[b, 32:64, BLK:] = rows[32:64]


def early_pairs(lists_ref):
    return jnp.minimum(lists_ref[4, 0] // GROUPS[-1] * GROUPS[-1], EARLY)


def first_kernel(
    blocks, packed_ref, seg_ref,
    lists, forces, source, target, comp,
    feat, counted, done,
):
    gather_components(seg_ref, comp, blocks)

    @pl.when(lax.axis_index("gz") == 0)
    def _():
        sort_pairs(blocks, packed_ref[...].reshape(1, packed_ref.shape[0]), lists)
        copy = pltpu.make_async_copy(lists, counted, done)
        copy.start()
        own_tables(blocks, comp, feat, source, target)
        forces[...] = jnp.zeros_like(forces)
        copy.wait()
        all_pairs(early_pairs(counted), lambda p: counted[0, p], target, source, forces, GROUPS[2:])


def near_kernel(
    blocks, packed_ref, near_ref, own_comp, early_lists, early_forces, early_source, early_target,
    forces_ref, target_ref, lists_ref,
    comp, feat, source, lists, done,
):
    early = lax.axis_index("gz") == 0
    copy = pltpu.make_async_copy(lists, lists_ref, done)

    @pl.when(early)
    def _():
        lists[...] = early_lists[...]
        copy.start()
        forces_ref[...] = early_forces[...]
        target_ref[...] = early_target[...]
        source[0:blocks] = early_source[...]

    @pl.when(jnp.logical_not(early))
    def _():
        sort_pairs(blocks, packed_ref[...].reshape(1, packed_ref.shape[0]), lists)
        copy.start()
        own_tables(blocks, own_comp, feat, source, target_ref)
        forces_ref[...] = jnp.zeros_like(forces_ref)

    gather_components(near_ref, comp, blocks)
    source_table(comp, feat, source, blocks, blocks)
    empty_block(source, 2 * blocks)
    copy.wait()
    base = jnp.where(early, early_pairs(lists_ref), 0)
    all_pairs(lists_ref[2, 0] - base, lambda p: lists_ref[0, base + p], target_ref, source, forces_ref)


def one_hot(at, row):
    return jnp.where(at == row, jnp.ones((), BF), jnp.zeros((), BF))


def span_of(targets):
    return -(-targets * (NODE_DEV // WIDE) // 8) * 8


def far_kernel(
    blocks, steps, lists_ref, far_ref, target_ref, comp_ref, near_forces,
    owner_ref, slot_ref, *rest,
):
    targets = 1 + 2 * len(set(steps))
    outs, (feat, source, forces, scaled, total_low, total_high) = rest[:targets], rest[targets:]
    source_table(far_ref, feat, source, 0, blocks)
    empty_block(source, blocks)
    forces[...] = near_forces[...]
    all_pairs(lists_ref[3, 0], lambda p: lists_ref[1, p], target_ref, source, forces)

    flat = forces.reshape(blocks * MOM, BLK)
    row = [flat[pl.ds(m, blocks, stride=MOM), :] for m in range(10)]
    for k in range(3):
        pulled = row[k] + row[3 + k] + row[6 + k]
        half = 0.5 * (comp_ref[k * blocks : (k + 1) * blocks, :] * row[9] - pulled)
        hi = half.astype(BF).astype(F32)
        scaled[k * blocks : (k + 1) * blocks, :] = hi
        scaled[(3 + k) * blocks : (4 + k) * blocks, :] = half - hi

    highs = NODE_DEV // WIDE
    span = span_of(targets)
    codes = owner_ref[...]
    column = lax.axis_index("col")
    place = jnp.zeros_like(codes)
    for n, step in enumerate(steps):
        to = 1 + 2 * steps.index(step)
        odd = (column // step) % 2
        place = jnp.where(codes == 1 + 2 * n, to + odd, place)
        place = jnp.where(codes == 2 + 2 * n, to + 1 - odd, place)
    slot = slot_ref[...]
    high = place * highs + slot // WIDE
    low = slot % WIDE
    high, low = high.astype(F32).astype(BF), low.astype(F32).astype(BF)
    high_at = lax.broadcasted_iota(jnp.int32, (span, BLK), 0).astype(F32).astype(BF)
    low_at = lax.broadcasted_iota(jnp.int32, (WIDE, BLK), 0).astype(F32).astype(BF)
    summed = None
    for first in range(0, blocks, 4):
        lefts, rights = [], []
        for b in range(first, first + 4):
            lanes = slice(b * BLK, (b + 1) * BLK)
            values = [scaled[m * blocks + b : m * blocks + b + 1, :].astype(BF) for m in range(6)]
            for end in range(2):
                rights.append(one_hot(low_at, low[end : end + 1, lanes]))
                hit = one_hot(high_at, high[end : end + 1, lanes])
                lefts.append(jnp.concatenate([hit * value for value in values], axis=0))
        part = lax.dot_general(
            jnp.concatenate(lefts, axis=1), jnp.concatenate(rights, axis=1), _NT, preferred_element_type=F32
        )
        summed = part if summed is None else summed + part
    summed = summed[: 3 * span] + summed[3 * span :]
    for half, total in enumerate((total_low, total_high)):
        total[...] = summed[:, half * BLK : (half + 1) * BLK]
    for t, out in enumerate(outs):
        for h in range(highs):
            for half, total in enumerate((total_low, total_high)):
                out[:, h * WIDE + half * BLK : h * WIDE + (half + 1) * BLK] = total[pl.ds(t * highs + h, 3, stride=span), :]


def swaps(peers, step, late):
    firsts = [i for i in range(peers) if (i // step) % 2 == late]
    return [(i, (i + step) % peers) for i in firsts] + [((i + step) % peers, i) for i in firsts]


def on_device(segments, node_owner, node_slot, pair_first, pair_second, pair_count):
    width = segments.shape[1]
    blocks = width // BLK
    slots = pair_first.shape[0]
    places = -(-(slots + GROUPS[0]) // BLK) * BLK
    peers = lax.axis_size("gz")
    smem = pl.BlockSpec(memory_space=pltpu.SMEM)
    vmem = pl.BlockSpec(memory_space=pltpu.VMEM)
    params = pltpu.CompilerParams(vmem_limit_bytes=40 << 20)

    near = lax.ppermute(segments, "gz", swaps(peers, 1, 0))

    odd = lax.axis_index("gz") % 2
    beyond = jnp.where(odd == 1, pair_second < blocks, pair_second >= 2 * blocks)
    own = jnp.logical_and(pair_second >= blocks, pair_second < 2 * blocks)
    region = jnp.where(own, 0, jnp.where(beyond, 1, 2))
    old = jnp.where(pair_second >= 2 * blocks, 2, jnp.where(pair_second >= blocks, 1, 0))
    renumbered = pair_second + (region - old) * blocks
    listed = jnp.arange(slots, dtype=jnp.int32) < pair_count[0]
    packed = jnp.where(listed, pair_first * 128 + renumbered, -1)

    early_shapes = (
        jax.ShapeDtypeStruct((8, places), jnp.int32),
        jax.ShapeDtypeStruct((blocks, MOM, BLK), F32),
        jax.ShapeDtypeStruct((blocks, ROWS, BLK), BF),
        jax.ShapeDtypeStruct((blocks, ROWS, 2 * BLK), BF),
        jax.ShapeDtypeStruct((9 * blocks, BLK), F32),
    )
    early = pl.pallas_call(
        functools.partial(first_kernel, blocks),
        out_shape=early_shapes,
        in_specs=[vmem, vmem],
        out_specs=(vmem,) * 5,
        scratch_shapes=[
            pltpu.VMEM((ROWS * blocks, BLK), F32),
            pltpu.SMEM((8, places), jnp.int32),
            pltpu.SemaphoreType.DMA,
        ],
        compiler_params=params,
    )(packed, segments)
    *early, comp = early
    far = lax.ppermute(comp, "gz", swaps(peers, 1, 1))

    forces, table, lists = pl.pallas_call(
        functools.partial(near_kernel, blocks),
        out_shape=(
            jax.ShapeDtypeStruct((blocks, MOM, BLK), F32),
            jax.ShapeDtypeStruct((blocks, ROWS, 2 * BLK), BF),
            jax.ShapeDtypeStruct((8, places), jnp.int32),
        ),
        in_specs=[vmem] * 7,
        out_specs=(vmem, vmem, smem),
        scratch_shapes=[
            pltpu.VMEM((9 * blocks, BLK), F32),
            pltpu.VMEM((ROWS * blocks, BLK), F32),
            pltpu.VMEM((2 * blocks + 1, ROWS, BLK), BF),
            pltpu.VMEM((8, places), jnp.int32),
            pltpu.SemaphoreType.DMA,
        ],
        compiler_params=params,
        cost_estimate=pl.CostEstimate(flops=10_000_000_000, bytes_accessed=1_000_000, transcendentals=0),
    )(packed, near, comp, *early)

    columns = lax.axis_size("col")
    steps = (1, columns // 4)
    distinct = list(dict.fromkeys(steps))
    targets = 1 + 2 * len(distinct)
    span = span_of(targets)
    partials = pl.pallas_call(
        functools.partial(far_kernel, blocks, steps),
        out_shape=tuple(jax.ShapeDtypeStruct((3, NODE_DEV), F32) for _ in range(targets)),
        in_specs=[smem] + [vmem] * 6,
        out_specs=(vmem,) * targets,
        scratch_shapes=[
            pltpu.VMEM((ROWS * blocks, BLK), F32),
            pltpu.VMEM((blocks + 1, ROWS, BLK), BF),
            pltpu.VMEM((blocks, MOM, BLK), F32),
            pltpu.VMEM((6 * blocks, BLK), F32),
            pltpu.VMEM((3 * span, BLK), F32),
            pltpu.VMEM((3 * span, BLK), F32),
        ],
        compiler_params=params,
    )(lists, far, table, comp, forces, node_owner, node_slot)
    node_total = partials[0]
    for n, partial in enumerate(partials[1:]):
        node_total = node_total + lax.ppermute(partial, "col", swaps(columns, distinct[n // 2], n % 2))
    return node_total


def solution(mesh):
    in_specs = (
        P(None, ("col", "gz")),
        P(None, ("col", "gz")),
        P(None, ("col", "gz")),
        P(("col", "gz")),
        P(("col", "gz")),
        P(("col", "gz")),
    )
    out_specs = P(None, ("col", "gz"))
    return jax.shard_map(
        on_device, mesh=mesh, in_specs=in_specs, out_specs=out_specs, check_vma=False
    )
```
